32 devices in a mesh: groups: 2 (over x), expert: 16 (over z, y, core).
Axes of the slice: x: 2, y: 2, z: 4, core: 2. Of those that a mesh axis runs over, the one named last changes fastest.
Arguments:
- output_gradient: bfloat16 [2048, 8192], P('expert', 'groups'), parts along dimension 1, may hold values from -4 to 4
- router_weight_table: bfloat16 [2048, 16], P('expert', 'groups'), parts along dimension 1, may hold values from 0.019897461 to 0.5
- routes: int32 [2048, 16], P('expert', 'groups'), parts along dimension 1, may hold values from 0 to 15, all different within a row; in each aligned block of 128 rows (0 to 127, 128 to 255, ...) at most 72 rows name the same one
- hidden: bfloat16 [16, 2304, 768], P('expert', 'groups'), parts along dimension 1, may hold values from -4 to 4
- down_weight_matrix: bfloat16 [16, 768, 4096], P('expert'), may hold values from -0.21875 to 0.21875
- adapter_first_factor: bfloat16 [16, 768, 16], P('expert'), may hold values from -0.21875 to 0.21875
- adapter_second_factor: bfloat16 [16, 16, 4096], P('expert'), may hold values from -1.5 to 1.5
Outputs:
- hidden_input_gradient: bfloat16 [16, 2304, 768], P('expert', 'groups'), parts along dimension 1
- adapter_first_gradient: float32 [16, 1536, 16], P('expert', 'groups'), parts along dimension 1
- adapter_second_gradient: float32 [16, 32, 4096], P('expert', 'groups'), parts along dimension 1
- router_weight_gradient: float32 [2048, 16], P('expert', 'groups'), parts along dimension 1
The draws below stay inside these ranges and needn't reach their ends.
There are 2 independent parts, one for each index of `groups`. The reference program is written for one: setup_inputs(seed, part) draws one part's arguments, and reference() takes and returns one part's arrays. A program takes and returns all parts, laid end to end along the dimension named above; an argument that names none is the same for every part. Nothing has to cross between parts.
Inputs may be any that keep to these rules, and one draw needn't show every extreme that they name: `routes`: each row names 8 different experts. Among the rows of one device no expert is named by more than 72 rows, and in some device's rows one expert is named by exactly 72.
All inputs are finite; a program needn't handle non-finite values.
Results may differ from the reference program's by a relative error of at most 0.0056.
Values may be sent and summed in bfloat16 or wider, within the bound.
A program may use at most 128 MiB of HBM per device.

```python
import math
import jax
import jax.numpy as jnp
import numpy as np
from jax import lax

HIDDEN_WIDTH = 4096
TOPK = 8
EXPERT_HIDDEN = 768
ADAPTER_RANK = 16
TOK_DEV = 128
EXPERT_TOTAL = 16
TOKENS = 2048
MOST = 72
CAP = 1152
N_EXPERT = 16


def steps_of(own_key, extent, pieces, smallest, top_value):
    gain, own = 1.0, jax.random.fold_in(own_key, 6)
    for axis_at, shards_of in pieces:
        draws = jnp.exp(jax.random.uniform(jax.random.fold_in(own, axis_at), (shards_of,), jnp.float32, smallest / len(pieces), top_value / len(pieces)))
        gain = gain * jnp.repeat(draws, extent[axis_at] // shards_of).reshape([-1 if axis == axis_at else 1 for axis in range(len(extent))])
    return gain


def assign_block(stream_key, own, number, rows, count, top, reach, slope):
    sequence = jax.random.permutation(stream_key, count)
    heavy_load, common = shares(count, rows * top, reach, slope, True), shares(count, rows * top, reach, slope, False)
    places = jnp.arange(count)

    def named(sizes, rotation):
        used = int((sizes > 0).sum())
        fixed = max(1, used // 4)
        shifted = fixed + (places - fixed + rotation * (used - fixed)) % max(1, count - fixed)
        return jnp.zeros((count,), jnp.int32).at[sequence[jnp.where(places < fixed, places, shifted)]].set(jnp.asarray(sizes, jnp.int32))

    sizes = jnp.where(number % 4 == 0, named(heavy_load, number // 4), named(common, number - number // 4 - 1))
    mixed = jax.random.permutation(jax.random.fold_in(own, 3), count)
    giver, receiver = mixed[0:count // 2 * 2:2], mixed[1:count // 2 * 2:2]
    margin = jnp.minimum(sizes[giver] - 1, reach - sizes[receiver]) // 2
    margin = jnp.where((giver == sequence[0]) | (receiver == sequence[0]) | (sizes[receiver] == 0), 0, jnp.maximum(margin, 0))
    shifted = jax.random.randint(jax.random.fold_in(own, 4), (count // 2,), 0, 1 << 20) % (margin + 1)
    sizes = sizes.at[giver].add(-shifted).at[receiver].add(shifted)
    labels = jnp.searchsorted(jnp.cumsum(sizes), jnp.arange(rows * top), side="right").astype(jnp.int32)
    table = labels.reshape(top, rows).T
    table = table[jax.random.permutation(jax.random.fold_in(own, 1), rows)]
    rotation = jax.random.randint(jax.random.fold_in(own, 2), (rows, 1), 0, top)
    return jnp.take_along_axis(table, (jnp.arange(top)[None, :] + rotation) % top, axis=1)


def shares(amount, total, most, slope, full):
    loads = [(1 << 20) // math.isqrt(rank ** slope) + 1 for rank in range(1, amount + 1)]
    largest = most if full else min(most, max(-(-total // amount), total * loads[0] // sum(loads)))
    least = 1 if total - largest >= amount - 1 else 0
    holding, spare = [largest] + [least] * (amount - 1), total - largest - least * (amount - 1)
    while spare > 0:
        movable = [i for i in range(1, amount) if holding[i] < largest] or [i for i in range(1, amount) if holding[i] < most]
        mass, left = sum([loads[i] for i in movable]), spare
        for i in movable:
            addition = min(most - holding[i], max(1, left * loads[i] // mass), spare)
            holding[i] = holding[i] + addition
            spare = spare - addition
    return np.array(holding)


def gaussian(rng, extent, deviation, reach, shards=(), kind=jnp.bfloat16):
    entries = deviation * jax.random.normal(rng, extent, jnp.float32)
    if shards:
        entries = entries * steps_of(rng, extent, shards, -0.22, 0.18)
    return jnp.clip(entries, -reach, reach).astype(kind)


def setup_inputs(seed: int = 0, part: int = 0) -> dict:
    seeds = jax.random.split(jax.random.key(seed), 8)
    part_splits = jax.random.split(jax.random.fold_in(seeds[7], part), 8)
    output_gradient = gaussian(part_splits[0], (TOKENS, HIDDEN_WIDTH), 0.5, 4.0, ((0, 16),))
    router_weight_table = jnp.clip(jnp.exp(math.log(0.5) - 3.224016 * jax.random.uniform(part_splits[1], (TOKENS, TOPK), jnp.float32) ** steps_of(part_splits[1], (TOKENS, TOPK), ((0, 16),), -0.2, 0.2)), 0.019897461, 0.5).astype(jnp.bfloat16)
    routes_keys = jax.random.split(jax.random.fold_in(part_splits[2], 1), TOKENS // TOK_DEV)
    routes_turns = jax.random.permutation(jax.random.fold_in(part_splits[2], 3), TOKENS // TOK_DEV)
    routes = jax.vmap(lambda own, number: assign_block(jax.random.fold_in(part_splits[2], 2), own, number, TOK_DEV, EXPERT_TOTAL, TOPK, MOST, 2))(routes_keys, routes_turns).reshape((TOKENS, TOPK))
    hidden = gaussian(part_splits[3], (EXPERT_TOTAL, CAP, EXPERT_HIDDEN), 0.5, 4.0, ((0, 16),))
    down_weight_matrix = gaussian(seeds[4], (EXPERT_TOTAL, EXPERT_HIDDEN, HIDDEN_WIDTH), EXPERT_HIDDEN ** -0.5, 0.21875, ((0, 16),))
    adapter_first_factor = gaussian(seeds[5], (EXPERT_TOTAL, EXPERT_HIDDEN, ADAPTER_RANK), EXPERT_HIDDEN ** -0.5, 0.21875, ((0, 16),))
    adapter_second_factor = gaussian(seeds[6], (EXPERT_TOTAL, ADAPTER_RANK, HIDDEN_WIDTH), ADAPTER_RANK ** -0.5, 1.5, ((0, 16),))
    return dict(output_gradient=output_gradient, router_weight_table=router_weight_table, routes=routes, hidden=hidden, down_weight_matrix=down_weight_matrix, adapter_first_factor=adapter_first_factor, adapter_second_factor=adapter_second_factor)


adapter_scale = 2.0


def reference(output_gradient, router_weight_table, routes, hidden, down_weight_matrix, adapter_first_factor, adapter_second_factor):
    expert_count = hidden.shape[0]
    blocks = routes.reshape(N_EXPERT, TOK_DEV, TOPK)
    member = jnp.sum((blocks[:, :, :, None] == jnp.arange(expert_count, dtype=jnp.int32)).astype(jnp.int32), axis=2)
    before = jnp.cumsum(member, axis=1) - member
    position = jnp.take_along_axis(before, blocks, axis=2).astype(jnp.int32)
    block_start = jnp.arange(N_EXPERT, dtype=jnp.int32)[:, None, None] * MOST
    cap_slot = (block_start + position).reshape(TOKENS, TOPK).astype(jnp.int32)
    token_ids = jnp.broadcast_to(jnp.arange(TOKENS, dtype=jnp.int32)[:, None], (TOKENS, TOPK))
    slot_token_index = jnp.full((expert_count, CAP), TOKENS, jnp.int32).at[routes, cap_slot].set(token_ids)
    slot_router_weight = jnp.zeros((expert_count, CAP), router_weight_table.dtype).at[routes, cap_slot].set(router_weight_table)
    padded = jnp.concatenate([output_gradient, jnp.zeros((1, HIDDEN_WIDTH), output_gradient.dtype)], axis=0)

    def single_expert(expert_entries):
        gathered_rows, expert_weight, hidden_activity, down_mapping, adapter_left_factor, adapter_right_factor = expert_entries
        slot_rows = padded[gathered_rows]
        scaled_gradient = (expert_weight.astype(jnp.float32)[:, None] * slot_rows.astype(jnp.float32)).astype(jnp.bfloat16)
        reduced_input = jnp.dot(hidden_activity, adapter_left_factor, preferred_element_type=jnp.float32).astype(jnp.bfloat16)
        expert_out = (jnp.dot(hidden_activity, down_mapping, preferred_element_type=jnp.float32)
                      + adapter_scale * jnp.dot(reduced_input, adapter_right_factor, preferred_element_type=jnp.float32)).astype(jnp.bfloat16)
        partial_products = jnp.sum(slot_rows.astype(jnp.float32) * expert_out.astype(jnp.float32), axis=1)
        reduced_gradient = jnp.dot(scaled_gradient, adapter_right_factor.T, preferred_element_type=jnp.float32).astype(jnp.bfloat16)
        grad_in = (jnp.dot(scaled_gradient, down_mapping.T, preferred_element_type=jnp.float32)
                   + adapter_scale * jnp.dot(reduced_gradient, adapter_left_factor.T, preferred_element_type=jnp.float32)).astype(jnp.bfloat16)
        left_factor_gradient = adapter_scale * jnp.dot(hidden_activity.T, reduced_gradient, preferred_element_type=jnp.float32)
        right_factor_gradient = adapter_scale * jnp.dot(reduced_input.T, scaled_gradient, preferred_element_type=jnp.float32)
        return grad_in, left_factor_gradient, right_factor_gradient, partial_products

    hidden_input_gradient, adapter_first_gradient, adapter_second_gradient, partial_products = lax.map(
        single_expert, (slot_token_index, slot_router_weight, hidden, down_weight_matrix, adapter_first_factor, adapter_second_factor))
    router_weight_gradient = partial_products[routes, cap_slot]
    return hidden_input_gradient, adapter_first_gradient, adapter_second_gradient, router_weight_gradient
```

```python
import functools

import jax
import jax.numpy as jnp
from jax import lax
from jax.experimental import pallas as pl
from jax.experimental.pallas import tpu as pltpu
from jax.sharding import PartitionSpec as P

adapter_scale = 2.0
MIB = 1 << 20


def dot(a, b, dims):
    return lax.dot_general(a, b, ((dims[:1], dims[1:]), ((), ())), preferred_element_type=jnp.float32)


def ring_kernel(
    peers,
    per_source,
    strip,
    grad_hbm,
    weight_ref,
    routes_ref,
    hidden_ref,
    down_hbm,
    first_ref,
    second_ref,
    out_ref,
    first_out,
    second_out,
    router_out,
    gathered,
    down,
    low_in,
    wide,
    thin,
    meta_out,
    meta_in,
    router_send,
    router_recv,
    right_send,
    right_recv,
    left_send,
    left_recv,
    pair_send,
    pair_recv,
    meta_send,
    meta_got,
    back_send,
    back_got,
    local_sem,
):
    tokens, width = grad_hbm.shape
    inner = hidden_ref.shape[1]
    top = routes_ref.shape[1]
    half = tokens // 2
    chips = peers // 2
    side = chips // 2
    slots = 2 * per_source
    far = chips // 2
    last = 2 * (far - 1)

    me = lax.axis_index("expert")
    core = lax.rem(me, 2)
    chip = lax.div(me, 2)
    row, column = lax.div(chip, 2), lax.rem(chip, 2)
    place = row + column * (chips - 1 - 2 * row)

    def chip_at(position):
        position = lax.rem(position + chips, chips)
        col = lax.div(position, side)
        return 2 * (position + col * (chips - 1 - 2 * position)) + col

    def device(index):
        return dict(device_id={"expert": index}, device_id_type=pl.DeviceIdType.MESH)

    right = 2 * chip_at(place + 1) + core
    left = 2 * chip_at(place - 1) + core
    sibling = chip * 2 + 1 - core

    barrier = pltpu.get_barrier_semaphore()
    for ahead in range(1, peers):
        pl.semaphore_signal(barrier, inc=1, **device(lax.rem(me + ahead, peers)))

    down_copy = pltpu.make_async_copy(down_hbm, down, local_sem.at[0])
    down_copy.start()
    own_copy = pltpu.make_async_copy(grad_hbm, gathered.at[chip, core], local_sem.at[1])
    own_copy.start()

    expert_at = lax.broadcasted_iota(jnp.int32, (tokens, peers), 1)
    member = jnp.zeros((tokens, peers), jnp.float32)
    table = jnp.zeros((tokens, peers), jnp.float32)
    for k in range(top):
        same = routes_ref[:, k : k + 1] == expert_at
        member += jnp.where(same, 1.0, 0.0)
        table += jnp.where(same, weight_ref[:, k : k + 1].astype(jnp.float32), 0.0)
    at0 = lax.broadcasted_iota(jnp.int32, (tokens, tokens), 0)
    at1 = lax.broadcasted_iota(jnp.int32, (tokens, tokens), 1)
    earlier = jnp.where(at0 < at1, 1.0, 0.0).astype(jnp.bfloat16)
    unit = jnp.where(at0 == at1, 1.0, 0.0).astype(jnp.bfloat16)
    member = member.astype(jnp.bfloat16)
    before = dot(member, earlier, (0, 0))
    position = jnp.where(dot(member, unit, (0, 0)) > 0.5, before, -1.0)
    weights = dot(table.astype(jnp.bfloat16), unit, (0, 0))
    meta_out[...] = jnp.zeros_like(meta_out)
    for e in range(peers):
        meta_out[e, 0:1, :] = position[e : e + 1, :]
        meta_out[e, 1:2, :] = weights[e : e + 1, :]

    pl.semaphore_wait(barrier, peers - 1)

    def rows(chunk):
        return pl.ds(chunk * half, half)

    def send_right(k):
        step, chunk = k // 2, k % 2
        target = gathered.at[chip_at(place - step), core, rows(chunk)]
        return pltpu.make_async_remote_copy(
            src_ref=grad_hbm.at[rows(chunk)] if step == 0 else target,
            dst_ref=target,
            send_sem=right_send.at[k],
            recv_sem=right_recv.at[k],
            **device(right),
        )

    def send_left(k):
        step, chunk = k // 2, 1 - k % 2
        target = gathered.at[chip_at(place + step), core, rows(chunk)]
        return pltpu.make_async_remote_copy(
            src_ref=grad_hbm.at[rows(chunk)] if step == 0 else target,
            dst_ref=target,
            send_sem=left_send.at[k],
            recv_sem=left_recv.at[k],
            **device(left),
        )

    def from_left(k):
        block = gathered.at[chip_at(place - 1 - k // 2), core, rows(k % 2)]
        return pltpu.make_async_remote_copy(
            src_ref=block, dst_ref=block, send_sem=right_send.at[k], recv_sem=right_recv.at[k],
            **device(left),
        )

    def from_right(k):
        block = gathered.at[chip_at(place + 1 + k // 2), core, rows(1 - k % 2)]
        return pltpu.make_async_remote_copy(
            src_ref=block, dst_ref=block, send_sem=left_send.at[k], recv_sem=left_recv.at[k],
            **device(right),
        )

    def pair_copy(number, block, source=None):
        return pltpu.make_async_remote_copy(
            src_ref=block if source is None else source,
            dst_ref=block,
            send_sem=pair_send.at[number],
            recv_sem=pair_recv.at[number],
            **device(sibling),
        )

    def pair_left(k, at_core):
        return pair_copy(1 + k, gathered.at[chip_at(place - 1 - k // 2), at_core, rows(k % 2)])

    def pair_right(k, at_core):
        block = gathered.at[chip_at(place + 1 + k // 2), at_core, rows(1 - k % 2)]
        return pair_copy(2 + last + k, block)

    for k in range(2):
        send_right(k).start()
        send_left(k).start()
    own_pair = pair_copy(0, gathered.at[chip, core], grad_hbm)
    own_pair.start()

    def meta_copy(target):
        return pltpu.make_async_remote_copy(
            src_ref=meta_out.at[target],
            dst_ref=meta_in.at[me],
            send_sem=meta_send.at[target],
            recv_sem=meta_got.at[me],
            **device(target),
        )

    def send_meta(ahead, carry):
        meta_copy(lax.rem(me + ahead, peers)).start()
        return carry

    lax.fori_loop(1, peers, send_meta, 0)
    meta_in[me] = meta_out[me]

    first_out[...] = jnp.zeros_like(first_out)
    second_out[...] = jnp.zeros_like(second_out)
    low_in[...] = dot(hidden_ref[...], first_ref[...], (1, 0)).astype(jnp.bfloat16)

    def wait_meta(ahead, carry):
        source = lax.rem(me + ahead, peers)
        pltpu.make_async_remote_copy(
            src_ref=meta_out.at[source],
            dst_ref=meta_in.at[source],
            send_sem=meta_send.at[source],
            recv_sem=meta_got.at[source],
            **device(source),
        ).wait()
        return carry

    lax.fori_loop(1, peers, wait_meta, 0)
    down_copy.wait()
    own_copy.wait()

    def back_copy(target):
        return pltpu.make_async_remote_copy(
            src_ref=router_send.at[target],
            dst_ref=router_recv.at[me],
            send_sem=back_send.at[target],
            recv_sem=back_got.at[me],
            **device(target),
        )

    def work(which):
        where = pl.ds(pl.multiple_of(which * slots, 16), slots)
        meta0, meta1 = meta_in[2 * which], meta_in[2 * which + 1]
        high = meta1[0:1, :]
        high = jnp.where(high < 0.0, -1.0, high + float(per_source))
        slot_of = jnp.concatenate([meta0[0:1, :], high], axis=1)
        weight = jnp.concatenate([meta0[1:2, :], meta1[1:2, :]], axis=1)
        slot_at = lax.broadcasted_iota(jnp.int32, (slots, 2 * tokens), 0).astype(jnp.float32)
        pick = jnp.where(slot_at == slot_of, 1.0, 0.0)
        slot_weight = jnp.sum(pick * weight, axis=1, keepdims=True)
        pick16 = pick.astype(jnp.bfloat16)
        hidden = hidden_ref[where, :]
        weighted = (slot_weight * low_in[where, :].astype(jnp.float32)).astype(jnp.bfloat16)
        mixed = dot(weighted, pick16, (0, 0)).astype(jnp.bfloat16)
        both = jnp.concatenate([pick16, mixed], axis=0)
        wide[...] = jnp.zeros_like(wide)
        thin[...] = jnp.zeros_like(thin)

        def strip_step(at, carry):
            lanes = pl.ds(pl.multiple_of(at * strip, strip), strip)
            block = gathered[which, :, :, lanes].reshape(2 * tokens, strip)
            product = dot(both, block, (1, 0))
            slot_rows = product[:slots].astype(jnp.bfloat16)
            second_out[:, lanes] += adapter_scale * product[slots:]
            wide[...] += dot(slot_rows, down[:, lanes], (1, 1))
            thin[...] += dot(slot_rows, second_ref[:, lanes], (1, 1))
            return carry

        lax.fori_loop(0, width // strip, strip_step, 0)
        low = thin[...]
        total = wide[...] + adapter_scale * dot(low.astype(jnp.bfloat16), first_ref[...], (1, 1))
        out_ref[where, :] = (slot_weight * total).astype(jnp.bfloat16)
        low_grad = (slot_weight * low).astype(jnp.bfloat16)
        first_out[...] += adapter_scale * dot(low_grad, hidden, (0, 0))
        router = jnp.sum(hidden.astype(jnp.float32) * total, axis=1, keepdims=True)
        routed = jnp.sum(pick * router, axis=0, keepdims=True)
        router_send[2 * which] = jnp.broadcast_to(routed[:, :tokens], (8, tokens))
        router_send[2 * which + 1] = jnp.broadcast_to(routed[:, tokens:], (8, tokens))

    def work_and_return(which):
        work(which)
        back_copy(2 * which).start()
        back_copy(2 * which + 1).start()

    for k in range(last + 1):
        from_left(k).wait_recv()
        if k + 2 <= last:
            send_right(k + 2).start()
        pair_left(k, core).start()
        from_right(k).wait_recv()
        if k + 2 <= last:
            send_left(k + 2).start()
        pair_right(k, core).start()
        if k == 0:
            pair_copy(0, gathered.at[chip, 1 - core]).wait_recv()
            work(chip)
            back_copy(sibling).start()
            router_recv[me] = router_send[me]
        elif k == last:
            pair_left(k, 1 - core).wait_recv()
            pair_right(k, 1 - core).wait_recv()
            work_and_return(chip_at(place + far))
        else:
            step = (k - 1) // 2
            if k % 2 == 1:
                for j in (2 * step, 2 * step + 1):
                    pair_left(j, 1 - core).wait_recv()
                work_and_return(chip_at(place - 1 - step))
            if k % 2 == 0 or k + 1 == last:
                for j in (2 * step, 2 * step + 1):
                    pair_right(j, 1 - core).wait_recv()
                work_and_return(chip_at(place + 1 + step))

    for k in range(last + 1):
        send_right(k).wait_send()
        send_left(k).wait_send()
        pair_left(k, core).wait_send()
        pair_right(k, core).wait_send()
    own_pair.wait_send()

    def wait_back(ahead, carry):
        source = lax.rem(me + ahead, peers)
        pltpu.make_async_remote_copy(
            src_ref=router_send.at[source],
            dst_ref=router_recv.at[source],
            send_sem=back_send.at[source],
            recv_sem=back_got.at[source],
            **device(source),
        ).wait()
        return carry

    lax.fori_loop(1, peers, wait_back, 0)
    router_out[...] = router_recv[...]


def ring_shards(
    output_gradient,
    router_weight_table,
    routes,
    hidden,
    down_weight_matrix,
    adapter_first_factor,
    adapter_second_factor,
):
    peers = lax.axis_size("expert")
    tokens, width = output_gradient.shape
    _, capacity, inner = hidden.shape
    rank = adapter_first_factor.shape[2]
    per_source = capacity // peers
    chips = peers // 2
    steps = 2 * (chips // 2 - 1) + 1
    strip = 1024 if width % 1024 == 0 else 128
    vmem = pl.BlockSpec(memory_space=pltpu.VMEM)
    hbm = pl.BlockSpec(memory_space=pl.ANY)
    dma = pltpu.SemaphoreType.DMA
    small = (peers, 8, tokens)
    grad, first, second, router = pl.pallas_call(
        functools.partial(ring_kernel, peers, per_source, strip),
        out_shape=(
            jax.ShapeDtypeStruct((capacity, inner), jnp.bfloat16),
            jax.ShapeDtypeStruct((rank, inner), jnp.float32),
            jax.ShapeDtypeStruct((rank, width), jnp.float32),
            jax.ShapeDtypeStruct(small, jnp.float32),
        ),
        in_specs=[hbm, vmem, vmem, vmem, hbm, vmem, vmem],
        out_specs=(vmem, vmem, vmem, vmem),
        scratch_shapes=[
            pltpu.VMEM((chips, 2, tokens, width), jnp.bfloat16),
            pltpu.VMEM((inner, width), jnp.bfloat16),
            pltpu.VMEM((capacity, rank), jnp.bfloat16),
            pltpu.VMEM((2 * per_source, inner), jnp.float32),
            pltpu.VMEM((2 * per_source, rank), jnp.float32),
            pltpu.VMEM(small, jnp.float32),
            pltpu.VMEM(small, jnp.float32),
            pltpu.VMEM(small, jnp.float32),
            pltpu.VMEM(small, jnp.float32),
            dma((steps,)),
            dma((steps,)),
            dma((steps,)),
            dma((steps,)),
            dma((2 * steps + 1,)),
            dma((2 * steps + 1,)),
            dma((peers,)),
            dma((peers,)),
            dma((peers,)),
            dma((peers,)),
            dma((2,)),
        ],
        compiler_params=pltpu.CompilerParams(
            collective_id=0, has_side_effects=True, vmem_limit_bytes=56 * MIB
        ),
    )(
        output_gradient,
        router_weight_table,
        routes,
        hidden[0],
        down_weight_matrix[0],
        adapter_first_factor[0],
        adapter_second_factor[0],
    )
    by_expert = router[:, 0, :].T
    chosen = routes[:, :, None] == jnp.arange(peers, dtype=jnp.int32)
    router_weight_gradient = jnp.sum(jnp.where(chosen, by_expert[:, None, :], 0.0), axis=2)
    return grad[None], first.T[None], second[None], router_weight_gradient


def ring_fits(peers, tokens_dev, width, experts, capacity, inner):
    per_source = capacity // peers
    gathered = peers * tokens_dev * width * 2
    return (
        experts == peers
        and peers >= 8
        and peers % 4 == 0
        and tokens_dev == 128
        and width % 128 == 0
        and inner % 128 == 0
        and (2 * per_source) % 16 == 0
        and gathered + inner * width * 2 + 3 * capacity * inner * 2 <= 40 * MIB
    )


def shards(
    output_gradient,
    router_weight_table,
    routes,
    hidden,
    down_weight_matrix,
    adapter_first_factor,
    adapter_second_factor,
):
    peer_count = lax.axis_size("expert")
    tokens_dev = output_gradient.shape[0]
    top_count = routes.shape[1]
    model_width = output_gradient.shape[1]
    exp_local = hidden.shape[0]
    capacity = hidden.shape[1]
    per_source = capacity // peer_count
    expert_count = exp_local * peer_count
    member = jnp.sum(
        (routes[:, :, None] == jnp.arange(expert_count, dtype=jnp.int32)).astype(jnp.bfloat16),
        axis=1,
    )
    lower_mask = (jnp.arange(tokens_dev)[:, None] > jnp.arange(tokens_dev)[None, :]).astype(
        jnp.bfloat16
    )
    before = jnp.dot(lower_mask, member, preferred_element_type=jnp.float32)
    position = jnp.take_along_axis(before, routes, axis=1).astype(jnp.int32)
    slot_index = (routes * per_source + position).reshape(-1)
    token_ids = jnp.repeat(jnp.arange(tokens_dev, dtype=jnp.int32), top_count)
    slot_token_index = (
        jnp.full((expert_count * per_source,), tokens_dev, jnp.int32).at[slot_index].set(token_ids)
    )
    slot_router_weight = (
        jnp.zeros((expert_count * per_source,), jnp.bfloat16)
        .at[slot_index]
        .set(router_weight_table.reshape(-1))
    )
    padded = jnp.concatenate(
        [output_gradient, jnp.zeros((1, model_width), output_gradient.dtype)], axis=0
    )
    send_rows = padded[slot_token_index]
    got_rows, got_weight = (
        lax.all_to_all(send_rows, "expert", split_axis=0, concat_axis=0, tiled=True),
        lax.all_to_all(slot_router_weight, "expert", split_axis=0, concat_axis=0, tiled=True),
    )
    slot_rows = (
        got_rows.reshape(peer_count, exp_local, per_source, model_width)
        .transpose(1, 0, 2, 3)
        .reshape(exp_local, capacity, model_width)
    )
    weight_rows = (
        got_weight.reshape(peer_count, exp_local, per_source)
        .transpose(1, 0, 2)
        .reshape(exp_local, capacity)
    )
    scaled_gradient = (
        weight_rows.astype(jnp.float32)[:, :, None] * slot_rows.astype(jnp.float32)
    ).astype(jnp.bfloat16)
    reduced_input = jnp.einsum(
        "onv,ovx->onx", hidden, adapter_first_factor, preferred_element_type=jnp.float32
    ).astype(jnp.bfloat16)
    joined_input = jnp.concatenate([hidden, reduced_input], axis=2)
    doubled_second = (adapter_scale * adapter_second_factor.astype(jnp.float32)).astype(
        jnp.bfloat16
    )
    joined_weight = jnp.concatenate([down_weight_matrix, doubled_second], axis=1)
    expert_out = jnp.einsum(
        "ecf,efd->ecd", joined_input, joined_weight, preferred_element_type=jnp.float32
    ).astype(jnp.bfloat16)
    partial_products = jnp.einsum(
        "ecd,ecd->ec", slot_rows, expert_out, preferred_element_type=jnp.float32
    )
    send_back = (
        partial_products.reshape(exp_local, peer_count, per_source).transpose(1, 0, 2).reshape(-1)
    )
    got_back = lax.all_to_all(send_back, "expert", split_axis=0, concat_axis=0, tiled=True)
    router_weight_gradient = got_back[slot_index].reshape(tokens_dev, top_count)
    reduced_gradient = jnp.einsum(
        "wzg,wvg->wzv", scaled_gradient, adapter_second_factor, preferred_element_type=jnp.float32
    ).astype(jnp.bfloat16)
    hidden_input_gradient = (
        jnp.einsum(
            "ecd,efd->ecf", scaled_gradient, down_weight_matrix, preferred_element_type=jnp.float32
        )
        + adapter_scale
        * jnp.einsum(
            "uvi,ubi->uvb",
            reduced_gradient,
            adapter_first_factor,
            preferred_element_type=jnp.float32,
        )
    ).astype(jnp.bfloat16)
    adapter_first_gradient = adapter_scale * jnp.einsum(
        "ecf,ecr->efr", hidden, reduced_gradient, preferred_element_type=jnp.float32
    )
    adapter_second_gradient = adapter_scale * jnp.einsum(
        "ecr,ecd->erd", reduced_input, scaled_gradient, preferred_element_type=jnp.float32
    )
    return (
        hidden_input_gradient,
        adapter_first_gradient,
        adapter_second_gradient,
        router_weight_gradient,
    )


def solution(mesh):
    in_specs = (
        P("expert", "groups"),
        P("expert", "groups"),
        P("expert", "groups"),
        P("expert", "groups", None),
        P("expert", None, None),
        P("expert", None, None),
        P("expert", None, None),
    )
    out_specs = (
        P("expert", "groups", None),
        P("expert", "groups", None),
        P("expert", "groups", None),
        P("expert", "groups"),
    )

    def call(*arrays):
        peers = mesh.shape["expert"]
        groups = mesh.shape["groups"]
        gradient, hidden = arrays[0], arrays[3]
        fits = ring_fits(
            peers,
            gradient.shape[0] // peers,
            gradient.shape[1] // groups,
            hidden.shape[0],
            hidden.shape[1] // groups,
            hidden.shape[2],
        )
        body = ring_shards if fits else shards
        return jax.shard_map(
            body, mesh=mesh, in_specs=in_specs, out_specs=out_specs, check_vma=False
        )(*arrays)

    return call
```

```python
import functools

import jax
import jax.numpy as jnp
from jax import lax
from jax.experimental import pallas as pl
from jax.experimental.pallas import tpu as pltpu
from jax.sharding import PartitionSpec as P

adapter_scale = 2.0
MIB = 1 << 20


def dot(a, b, dims):
    return lax.dot_general(a, b, ((dims[:1], dims[1:]), ((), ())), preferred_element_type=jnp.float32)


def ring_kernel(
    peers,
    per_source,
    strip,
    parts,
    grad_hbm,
    weight_ref,
    routes_ref,
    hidden_hbm,
    down_hbm,
    first_ref,
    second_ref,
    out_hbm,
    first_out,
    second_out,
    router_out,
    gathered,
    down,
    hidden_ref,
    out_ref,
    low_in,
    wide,
    thin,
    meta_out,
    meta_in,
    router_send,
    router_recv,
    right_send,
    right_recv,
    left_send,
    left_recv,
    pair_send,
    pair_recv,
    meta_send,
    meta_got,
    back_send,
    back_got,
    local_sem,
    out_sem,
):
    tokens, width = grad_hbm.shape
    inner = hidden_ref.shape[1]
    top = routes_ref.shape[0]
    piece = width // parts
    chips = peers // 2
    side = chips // 2
    slots = 2 * per_source
    far = chips // 2
    last = parts * (far - 1) + parts // 2 - 1

    me = lax.axis_index("expert")
    core = lax.rem(me, 2)
    chip = lax.div(me, 2)
    row, column = lax.div(chip, 2), lax.rem(chip, 2)
    place = row + column * (chips - 1 - 2 * row)

    def chip_at(position):
        position = lax.rem(position + chips, chips)
        col = lax.div(position, side)
        return 2 * (position + col * (chips - 1 - 2 * position)) + col

    def device(index):
        return dict(device_id={"expert": index}, device_id_type=pl.DeviceIdType.MESH)

    right = 2 * chip_at(place + 1) + core
    left = 2 * chip_at(place - 1) + core
    sibling = chip * 2 + 1 - core

    barrier = pltpu.get_barrier_semaphore()
    for ahead in range(1, peers):
        pl.semaphore_signal(barrier, inc=1, **device(lax.rem(me + ahead, peers)))

    down_copy = pltpu.make_async_copy(down_hbm, down, local_sem.at[0])
    down_copy.start()
    own_copy = pltpu.make_async_copy(grad_hbm, gathered.at[chip, core], local_sem.at[1])
    own_copy.start()
    hidden_copy = pltpu.make_async_copy(hidden_hbm, hidden_ref, local_sem.at[2])
    hidden_copy.start()

    expert_at = lax.broadcasted_iota(jnp.int32, (peers, tokens), 0)
    member = jnp.zeros((peers, tokens), jnp.float32)
    weights = jnp.zeros((peers, tokens), jnp.float32)
    for k in range(top):
        same = routes_ref[k : k + 1, :] == expert_at
        member += jnp.where(same, 1.0, 0.0)
        weights += jnp.where(same, weight_ref[k : k + 1, :].astype(jnp.float32), 0.0)
    at0 = lax.broadcasted_iota(jnp.int32, (tokens, tokens), 0)
    at1 = lax.broadcasted_iota(jnp.int32, (tokens, tokens), 1)
    earlier = jnp.where(at0 < at1, 1.0, 0.0).astype(jnp.bfloat16)
    before = dot(member.astype(jnp.bfloat16), earlier, (1, 0))
    position = jnp.where(member > 0.5, before, -1.0)
    meta_out[...] = jnp.zeros_like(meta_out)
    for e in range(peers):
        meta_out[e, 0:1, :] = position[e : e + 1, :]
        meta_out[e, 1:2, :] = weights[e : e + 1, :]

    pl.semaphore_wait(barrier, peers - 1)

    def lanes_of(chunk):
        return pl.ds(chunk * piece, piece)

    def send_right(k):
        step, chunk = k // parts, k % parts
        target = gathered.at[chip_at(place - step), core, :, lanes_of(chunk)]
        return pltpu.make_async_remote_copy(
            src_ref=grad_hbm.at[:, lanes_of(chunk)] if step == 0 else target,
            dst_ref=target,
            send_sem=right_send.at[k],
            recv_sem=right_recv.at[k],
            **device(right),
        )

    def send_left(k):
        step, chunk = k // parts, parts - 1 - k % parts
        target = gathered.at[chip_at(place + step), core, :, lanes_of(chunk)]
        return pltpu.make_async_remote_copy(
            src_ref=grad_hbm.at[:, lanes_of(chunk)] if step == 0 else target,
            dst_ref=target,
            send_sem=left_send.at[k],
            recv_sem=left_recv.at[k],
            **device(left),
        )

    def from_left(k):
        block = gathered.at[chip_at(place - 1 - k // parts), core, :, lanes_of(k % parts)]
        return pltpu.make_async_remote_copy(
            src_ref=block, dst_ref=block, send_sem=right_send.at[k], recv_sem=right_recv.at[k],
            **device(left),
        )

    def from_right(k):
        block = gathered.at[chip_at(place + 1 + k // parts), core, :, lanes_of(parts - 1 - k % parts)]
        return pltpu.make_async_remote_copy(
            src_ref=block, dst_ref=block, send_sem=left_send.at[k], recv_sem=left_recv.at[k],
            **device(right),
        )

    def pair_copy(number, block, source=None):
        return pltpu.make_async_remote_copy(
            src_ref=block if source is None else source,
            dst_ref=block,
            send_sem=pair_send.at[number],
            recv_sem=pair_recv.at[number],
            **device(sibling),
        )

    def pair_left(k, at_core):
        block = gathered.at[chip_at(place - 1 - k // parts), at_core, :, lanes_of(k % parts)]
        return pair_copy(1 + k, block)

    def pair_right(k, at_core):
        block = gathered.at[chip_at(place + 1 + k // parts), at_core, :, lanes_of(parts - 1 - k % parts)]
        return pair_copy(2 + last + k, block)

    for k in range(parts):
        send_right(k).start()
        send_left(k).start()
    own_pair = pair_copy(0, gathered.at[chip, core], grad_hbm)
    own_pair.start()

    def meta_copy(target):
        return pltpu.make_async_remote_copy(
            src_ref=meta_out.at[target],
            dst_ref=meta_in.at[me],
            send_sem=meta_send.at[target],
            recv_sem=meta_got.at[me],
            **device(target),
        )

    def send_meta(ahead, carry):
        meta_copy(lax.rem(me + ahead, peers)).start()
        return carry

    lax.fori_loop(1, peers, send_meta, 0)
    meta_in[me] = meta_out[me]

    first_out[...] = jnp.zeros_like(first_out)
    second_out[...] = jnp.zeros_like(second_out)
    hidden_copy.wait()
    low_in[...] = dot(hidden_ref[...], first_ref[...], (1, 1)).astype(jnp.bfloat16)

    def wait_meta(ahead, carry):
        source = lax.rem(me + ahead, peers)
        pltpu.make_async_remote_copy(
            src_ref=meta_out.at[source],
            dst_ref=meta_in.at[source],
            send_sem=meta_send.at[source],
            recv_sem=meta_got.at[source],
            **device(source),
        ).wait()
        return carry

    lax.fori_loop(1, peers, wait_meta, 0)
    down_copy.wait()
    own_copy.wait()

    def back_copy(target):
        return pltpu.make_async_remote_copy(
            src_ref=router_send.at[target],
            dst_ref=router_recv.at[me],
            send_sem=back_send.at[target],
            recv_sem=back_got.at[me],
            **device(target),
        )

    def out_copy(which):
        where = pl.ds(pl.multiple_of(which * slots, 16), slots)
        return pltpu.make_async_copy(out_ref.at[where, :], out_hbm.at[where, :], out_sem.at[which])

    def work(which):
        where = pl.ds(pl.multiple_of(which * slots, 16), slots)
        meta0, meta1 = meta_in[2 * which], meta_in[2 * which + 1]
        high = meta1[0:1, :]
        high = jnp.where(high < 0.0, -1.0, high + float(per_source))
        slot_of = jnp.concatenate([meta0[0:1, :], high], axis=1)
        weight = jnp.concatenate([meta0[1:2, :], meta1[1:2, :]], axis=1)
        slot_at = lax.broadcasted_iota(jnp.int32, (slots, 2 * tokens), 0).astype(jnp.float32)
        pick = jnp.where(slot_at == slot_of, 1.0, 0.0)
        slot_weight = jnp.sum(pick * weight, axis=1, keepdims=True)
        pick16 = pick.astype(jnp.bfloat16)
        hidden = hidden_ref[where, :]
        weighted = (slot_weight * low_in[where, :].astype(jnp.float32)).astype(jnp.bfloat16)
        mixed = dot(weighted, pick16, (0, 0)).astype(jnp.bfloat16)
        both = jnp.concatenate([pick16, mixed], axis=0)
        wide[...] = jnp.zeros_like(wide)
        thin[...] = jnp.zeros_like(thin)

        def strip_step(at, carry):
            lanes = pl.ds(pl.multiple_of(at * strip, strip), strip)
            block = gathered[which, :, :, lanes].reshape(2 * tokens, strip)
            product = dot(both, block, (1, 0))
            slot_rows = product[:slots].astype(jnp.bfloat16)
            second_out[:, lanes] += adapter_scale * product[slots:]
            wide[...] += dot(slot_rows, down[:, lanes], (1, 1))
            thin[...] += dot(slot_rows, second_ref[:, lanes], (1, 1))
            return carry

        lax.fori_loop(0, width // strip, strip_step, 0)
        low = thin[...]
        total = wide[...] + adapter_scale * dot(low.astype(jnp.bfloat16), first_ref[...], (1, 0))
        out_ref[where, :] = (slot_weight * total).astype(jnp.bfloat16)
        out_copy(which).start()
        low_grad = (slot_weight * low).astype(jnp.bfloat16)
        first_out[...] += adapter_scale * dot(low_grad, hidden, (0, 0))
        router = jnp.sum(hidden.astype(jnp.float32) * total, axis=1, keepdims=True)
        routed = jnp.sum(pick * router, axis=0, keepdims=True)
        router_send[2 * which] = jnp.broadcast_to(routed[:, :tokens], (8, tokens))
        router_send[2 * which + 1] = jnp.broadcast_to(routed[:, tokens:], (8, tokens))

    def work_and_return(which):
        work(which)
        back_copy(2 * which).start()
        back_copy(2 * which + 1).start()

    def wait_left(step, count):
        for k in range(parts * step, parts * step + count):
            pair_left(k, 1 - core).wait_recv()

    def wait_right(step, count):
        for k in range(parts * step, parts * step + count):
            pair_right(k, 1 - core).wait_recv()

    for k in range(last + 1):
        from_left(k).wait_recv()
        if k + parts <= last:
            send_right(k + parts).start()
        pair_left(k, core).start()
        from_right(k).wait_recv()
        if k + parts <= last:
            send_left(k + parts).start()
        pair_right(k, core).start()
        if k == 0:
            pair_copy(0, gathered.at[chip, 1 - core]).wait_recv()
            work(chip)
            back_copy(sibling).start()
            router_recv[me] = router_send[me]
        step = (k + 1) // parts - 1
        if k % parts == parts - 1:
            wait_left(step, parts)
            work_and_return(chip_at(place - 1 - step))
        if (k % parts == 0 and k > 0 and k < last) or (k + 1 == last and k % parts == parts - 1):
            if k % parts == 0:
                step = k // parts - 1
            wait_right(step, parts)
            work_and_return(chip_at(place + 1 + step))
        if k == last:
            wait_left(far - 1, parts // 2)
            wait_right(far - 1, parts // 2)
            work_and_return(chip_at(place + far))

    for k in range(last + 1):
        send_right(k).wait_send()
        send_left(k).wait_send()
        pair_left(k, core).wait_send()
        pair_right(k, core).wait_send()
    own_pair.wait_send()

    def wait_back(ahead, carry):
        source = lax.rem(me + ahead, peers)
        pltpu.make_async_remote_copy(
            src_ref=router_send.at[source],
            dst_ref=router_recv.at[source],
            send_sem=back_send.at[source],
            recv_sem=back_got.at[source],
            **device(source),
        ).wait()
        return carry

    lax.fori_loop(1, peers, wait_back, 0)
    returned = router_recv[:, 0, :]
    for k in range(top):
        same = routes_ref[k : k + 1, :] == expert_at
        router_out[k : k + 1, :] = jnp.sum(jnp.where(same, returned, 0.0), axis=0, keepdims=True)
    for which in range(chips):
        out_copy(which).wait()


def ring_shards(
    output_gradient,
    router_weight_table,
    routes,
    hidden,
    down_weight_matrix,
    adapter_first_factor,
    adapter_second_factor,
):
    peers = lax.axis_size("expert")
    tokens, width = output_gradient.shape
    _, capacity, inner = hidden.shape
    rank = adapter_first_factor.shape[2]
    per_source = capacity // peers
    chips = peers // 2
    parts = 4
    steps = parts * (chips // 2 - 1) + parts // 2
    top = routes.shape[1]
    strip = 1024
    vmem = pl.BlockSpec(memory_space=pltpu.VMEM)
    hbm = pl.BlockSpec(memory_space=pl.ANY)
    dma = pltpu.SemaphoreType.DMA
    small = (peers, 8, tokens)
    grad, first, second, router = pl.pallas_call(
        functools.partial(ring_kernel, peers, per_source, strip, parts),
        out_shape=(
            jax.ShapeDtypeStruct((capacity, inner), jnp.bfloat16),
            jax.ShapeDtypeStruct((rank, inner), jnp.float32),
            jax.ShapeDtypeStruct((rank, width), jnp.float32),
            jax.ShapeDtypeStruct((top, tokens), jnp.float32),
        ),
        in_specs=[hbm, vmem, vmem, hbm, hbm, vmem, vmem],
        out_specs=(hbm, vmem, vmem, vmem),
        scratch_shapes=[
            pltpu.VMEM((chips, 2, tokens, width), jnp.bfloat16),
            pltpu.VMEM((inner, width), jnp.bfloat16),
            pltpu.VMEM((capacity, inner), jnp.bfloat16),
            pltpu.VMEM((capacity, inner), jnp.bfloat16),
            pltpu.VMEM((capacity, rank), jnp.bfloat16),
            pltpu.VMEM((2 * per_source, inner), jnp.float32),
            pltpu.VMEM((2 * per_source, rank), jnp.float32),
            pltpu.VMEM(small, jnp.float32),
            pltpu.VMEM(small, jnp.float32),
            pltpu.VMEM(small, jnp.float32),
            pltpu.VMEM(small, jnp.float32),
            dma((steps,)),
            dma((steps,)),
            dma((steps,)),
            dma((steps,)),
            dma((2 * steps + 1,)),
            dma((2 * steps + 1,)),
            dma((peers,)),
            dma((peers,)),
            dma((peers,)),
            dma((peers,)),
            dma((3,)),
            dma((chips,)),
        ],
        compiler_params=pltpu.CompilerParams(
            collective_id=0, has_side_effects=True, vmem_limit_bytes=56 * MIB
        ),
    )(
        output_gradient,
        router_weight_table.T,
        routes.T,
        hidden[0],
        down_weight_matrix[0],
        adapter_first_factor[0].T,
        adapter_second_factor[0],
    )
    return grad[None], first.T[None], second[None], router.T


def ring_fits(peers, tokens_dev, width, experts, capacity, inner):
    per_source = capacity // peers
    gathered = peers * tokens_dev * width * 2
    return (
        experts == peers
        and peers >= 8
        and peers % 4 == 0
        and tokens_dev == 128
        and width % 1024 == 0
        and inner % 128 == 0
        and (2 * per_source) % 16 == 0
        and gathered + inner * width * 2 + 3 * capacity * inner * 2 <= 40 * MIB
    )


def shards(
    output_gradient,
    router_weight_table,
    routes,
    hidden,
    down_weight_matrix,
    adapter_first_factor,
    adapter_second_factor,
):
    peer_count = lax.axis_size("expert")
    tokens_dev = output_gradient.shape[0]
    top_count = routes.shape[1]
    model_width = output_gradient.shape[1]
    exp_local = hidden.shape[0]
    capacity = hidden.shape[1]
    per_source = capacity // peer_count
    expert_count = exp_local * peer_count
    member = jnp.sum(
        (routes[:, :, None] == jnp.arange(expert_count, dtype=jnp.int32)).astype(jnp.bfloat16),
        axis=1,
    )
    lower_mask = (jnp.arange(tokens_dev)[:, None] > jnp.arange(tokens_dev)[None, :]).astype(
        jnp.bfloat16
    )
    before = jnp.dot(lower_mask, member, preferred_element_type=jnp.float32)
    position = jnp.take_along_axis(before, routes, axis=1).astype(jnp.int32)
    slot_index = (routes * per_source + position).reshape(-1)
    token_ids = jnp.repeat(jnp.arange(tokens_dev, dtype=jnp.int32), top_count)
    slot_token_index = (
        jnp.full((expert_count * per_source,), tokens_dev, jnp.int32).at[slot_index].set(token_ids)
    )
    slot_router_weight = (
        jnp.zeros((expert_count * per_source,), jnp.bfloat16)
        .at[slot_index]
        .set(router_weight_table.reshape(-1))
    )
    padded = jnp.concatenate(
        [output_gradient, jnp.zeros((1, model_width), output_gradient.dtype)], axis=0
    )
    send_rows = padded[slot_token_index]
    got_rows, got_weight = (
        lax.all_to_all(send_rows, "expert", split_axis=0, concat_axis=0, tiled=True),
        lax.all_to_all(slot_router_weight, "expert", split_axis=0, concat_axis=0, tiled=True),
    )
    slot_rows = (
        got_rows.reshape(peer_count, exp_local, per_source, model_width)
        .transpose(1, 0, 2, 3)
        .reshape(exp_local, capacity, model_width)
    )
    weight_rows = (
        got_weight.reshape(peer_count, exp_local, per_source)
        .transpose(1, 0, 2)
        .reshape(exp_local, capacity)
    )
    scaled_gradient = (
        weight_rows.astype(jnp.float32)[:, :, None] * slot_rows.astype(jnp.float32)
    ).astype(jnp.bfloat16)
    reduced_input = jnp.einsum(
        "onv,ovx->onx", hidden, adapter_first_factor, preferred_element_type=jnp.float32
    ).astype(jnp.bfloat16)
    joined_input = jnp.concatenate([hidden, reduced_input], axis=2)
    doubled_second = (adapter_scale * adapter_second_factor.astype(jnp.float32)).astype(
        jnp.bfloat16
    )
    joined_weight = jnp.concatenate([down_weight_matrix, doubled_second], axis=1)
    expert_out = jnp.einsum(
        "ecf,efd->ecd", joined_input, joined_weight, preferred_element_type=jnp.float32
    ).astype(jnp.bfloat16)
    partial_products = jnp.einsum(
        "ecd,ecd->ec", slot_rows, expert_out, preferred_element_type=jnp.float32
    )
    send_back = (
        partial_products.reshape(exp_local, peer_count, per_source).transpose(1, 0, 2).reshape(-1)
    )
    got_back = lax.all_to_all(send_back, "expert", split_axis=0, concat_axis=0, tiled=True)
    router_weight_gradient = got_back[slot_index].reshape(tokens_dev, top_count)
    reduced_gradient = jnp.einsum(
        "wzg,wvg->wzv", scaled_gradient, adapter_second_factor, preferred_element_type=jnp.float32
    ).astype(jnp.bfloat16)
    hidden_input_gradient = (
        jnp.einsum(
            "ecd,efd->ecf", scaled_gradient, down_weight_matrix, preferred_element_type=jnp.float32
        )
        + adapter_scale
        * jnp.einsum(
            "uvi,ubi->uvb",
            reduced_gradient,
            adapter_first_factor,
            preferred_element_type=jnp.float32,
        )
    ).astype(jnp.bfloat16)
    adapter_first_gradient = adapter_scale * jnp.einsum(
        "ecf,ecr->efr", hidden, reduced_gradient, preferred_element_type=jnp.float32
    )
    adapter_second_gradient = adapter_scale * jnp.einsum(
        "ecr,ecd->erd", reduced_input, scaled_gradient, preferred_element_type=jnp.float32
    )
    return (
        hidden_input_gradient,
        adapter_first_gradient,
        adapter_second_gradient,
        router_weight_gradient,
    )


def solution(mesh):
    in_specs = (
        P("expert", "groups"),
        P("expert", "groups"),
        P("expert", "groups"),
        P("expert", "groups", None),
        P("expert", None, None),
        P("expert", None, None),
        P("expert", None, None),
    )
    out_specs = (
        P("expert", "groups", None),
        P("expert", "groups", None),
        P("expert", "groups", None),
        P("expert", "groups"),
    )

    def call(*arrays):
        peers = mesh.shape["expert"]
        groups = mesh.shape["groups"]
        gradient, hidden = arrays[0], arrays[3]
        fits = ring_fits(
            peers,
            gradient.shape[0] // peers,
            gradient.shape[1] // groups,
            hidden.shape[0],
            hidden.shape[1] // groups,
            hidden.shape[2],
        )
        body = ring_shards if fits else shards
        return jax.shard_map(
            body, mesh=mesh, in_specs=in_specs, out_specs=out_specs, check_vma=False
        )(*arrays)

    return call
```

```python
import functools

import jax
import jax.numpy as jnp
from jax import lax
from jax.experimental import pallas as pl
from jax.experimental.pallas import tpu as pltpu
from jax.sharding import PartitionSpec as P

adapter_scale = 2.0
MIB = 1 << 20


def dot(a, b, dims):
    return lax.dot_general(a, b, ((dims[:1], dims[1:]), ((), ())), preferred_element_type=jnp.float32)


def ring_kernel(
    peers,
    per_source,
    strip,
    parts,
    grad_hbm,
    weight_ref,
    routes_ref,
    hidden_hbm,
    down_hbm,
    first_ref,
    second_ref,
    out_hbm,
    first_out,
    second_out,
    router_out,
    gathered,
    down,
    hidden_ref,
    out_ref,
    low_in,
    wide,
    thin,
    meta,
    router_send,
    router_recv,
    right_send,
    right_recv,
    left_send,
    left_recv,
    pair_send,
    pair_recv,
    meta_right_send,
    meta_right_recv,
    meta_left_send,
    meta_left_recv,
    meta_pair_send,
    meta_pair_recv,
    back_send,
    back_got,
    local_sem,
    out_sem,
):
    tokens, width = grad_hbm.shape
    inner = hidden_ref.shape[1]
    top = routes_ref.shape[0]
    piece = width // parts
    chips = peers // 2
    side = chips // 2
    slots = 2 * per_source
    far = chips // 2
    last = parts * (far - 1) + parts // 2 - 1

    me = lax.axis_index("expert")
    core = lax.rem(me, 2)
    chip = lax.div(me, 2)
    row, column = lax.div(chip, 2), lax.rem(chip, 2)
    place = row + column * (chips - 1 - 2 * row)

    def chip_at(position):
        position = lax.rem(position + chips, chips)
        col = lax.div(position, side)
        return 2 * (position + col * (chips - 1 - 2 * position)) + col

    def device(index):
        return dict(device_id={"expert": index}, device_id_type=pl.DeviceIdType.MESH)

    right = 2 * chip_at(place + 1) + core
    left = 2 * chip_at(place - 1) + core
    sibling = chip * 2 + 1 - core

    barrier = pltpu.get_barrier_semaphore()
    for other in (right, left, sibling):
        pl.semaphore_signal(barrier, inc=1, **device(other))

    down_copy = pltpu.make_async_copy(down_hbm, down, local_sem.at[0])
    down_copy.start()
    own_copy = pltpu.make_async_copy(grad_hbm, gathered.at[chip, core], local_sem.at[1])
    own_copy.start()
    hidden_copy = pltpu.make_async_copy(hidden_hbm, hidden_ref, local_sem.at[2])
    hidden_copy.start()

    expert_at = lax.broadcasted_iota(jnp.int32, (peers, tokens), 0)
    member = jnp.zeros((peers, tokens), jnp.float32)
    weights = jnp.zeros((peers, tokens), jnp.float32)
    for k in range(top):
        same = routes_ref[k : k + 1, :] == expert_at
        member += jnp.where(same, 1.0, 0.0)
        weights += jnp.where(same, weight_ref[k : k + 1, :].astype(jnp.float32), 0.0)
    at0 = lax.broadcasted_iota(jnp.int32, (tokens, tokens), 0)
    at1 = lax.broadcasted_iota(jnp.int32, (tokens, tokens), 1)
    earlier = jnp.where(at0 < at1, 1.0, 0.0).astype(jnp.bfloat16)
    before = dot(member.astype(jnp.bfloat16), earlier, (1, 0))
    position = jnp.where(member > 0.5, before, -1.0)
    meta[chip, core] = jnp.concatenate([position, weights], axis=0)

    pl.semaphore_wait(barrier, 3)

    def lanes_of(chunk):
        return pl.ds(chunk * piece, piece)

    def send_right(k):
        step, chunk = k // parts, k % parts
        target = gathered.at[chip_at(place - step), core, :, lanes_of(chunk)]
        return pltpu.make_async_remote_copy(
            src_ref=grad_hbm.at[:, lanes_of(chunk)] if step == 0 else target,
            dst_ref=target,
            send_sem=right_send.at[k],
            recv_sem=right_recv.at[k],
            **device(right),
        )

    def send_left(k):
        step, chunk = k // parts, parts - 1 - k % parts
        target = gathered.at[chip_at(place + step), core, :, lanes_of(chunk)]
        return pltpu.make_async_remote_copy(
            src_ref=grad_hbm.at[:, lanes_of(chunk)] if step == 0 else target,
            dst_ref=target,
            send_sem=left_send.at[k],
            recv_sem=left_recv.at[k],
            **device(left),
        )

    def from_left(k):
        block = gathered.at[chip_at(place - 1 - k // parts), core, :, lanes_of(k % parts)]
        return pltpu.make_async_remote_copy(
            src_ref=block, dst_ref=block, send_sem=right_send.at[k], recv_sem=right_recv.at[k],
            **device(left),
        )

    def from_right(k):
        block = gathered.at[chip_at(place + 1 + k // parts), core, :, lanes_of(parts - 1 - k % parts)]
        return pltpu.make_async_remote_copy(
            src_ref=block, dst_ref=block, send_sem=left_send.at[k], recv_sem=left_recv.at[k],
            **device(right),
        )

    def pair_copy(number, block, source=None):
        return pltpu.make_async_remote_copy(
            src_ref=block if source is None else source,
            dst_ref=block,
            send_sem=pair_send.at[number],
            recv_sem=pair_recv.at[number],
            **device(sibling),
        )

    def pair_left(k, at_core):
        block = gathered.at[chip_at(place - 1 - k // parts), at_core, :, lanes_of(k % parts)]
        return pair_copy(1 + k, block)

    def pair_right(k, at_core):
        block = gathered.at[chip_at(place + 1 + k // parts), at_core, :, lanes_of(parts - 1 - k % parts)]
        return pair_copy(2 + last + k, block)

    def meta_copy(block, send, recv, target):
        return pltpu.make_async_remote_copy(
            src_ref=block, dst_ref=block, send_sem=send, recv_sem=recv, **device(target)
        )

    def meta_right(step, origin):
        block = meta.at[chip_at(origin), core]
        return meta_copy(block, meta_right_send.at[step], meta_right_recv.at[step], right)

    def meta_left(step, origin):
        block = meta.at[chip_at(origin), core]
        return meta_copy(block, meta_left_send.at[step], meta_left_recv.at[step], left)

    def meta_pair(number, origin, at_core):
        block = meta.at[chip_at(origin), at_core]
        return meta_copy(block, meta_pair_send.at[number], meta_pair_recv.at[number], sibling)

    meta_right(0, place).start()
    meta_left(0, place).start()
    meta_pair(0, place, core).start()
    for k in range(parts):
        send_right(k).start()
        send_left(k).start()
    own_pair = pair_copy(0, gathered.at[chip, core], grad_hbm)
    own_pair.start()

    first_out[...] = jnp.zeros_like(first_out)
    second_out[...] = jnp.zeros_like(second_out)
    hidden_copy.wait()
    low_in[...] = dot(hidden_ref[...], first_ref[...], (1, 1)).astype(jnp.bfloat16)

    down_copy.wait()
    own_copy.wait()

    def back_copy(target):
        return pltpu.make_async_remote_copy(
            src_ref=router_send.at[target],
            dst_ref=router_recv.at[me],
            send_sem=back_send.at[target],
            recv_sem=back_got.at[me],
            **device(target),
        )

    def out_copy(which):
        where = pl.ds(pl.multiple_of(which * slots, 16), slots)
        return pltpu.make_async_copy(out_ref.at[where, :], out_hbm.at[where, :], out_sem.at[which])

    def begin(which):
        where = pl.ds(pl.multiple_of(which * slots, 16), slots)
        mine = lax.broadcasted_iota(jnp.int32, (peers, tokens), 0) == me

        def own_row(at_core, start):
            table = meta[which, at_core, start : start + peers, :]
            return jnp.sum(jnp.where(mine, table, 0.0), axis=0, keepdims=True)

        high = own_row(1, 0)
        high = jnp.where(high < 0.0, -1.0, high + float(per_source))
        slot_of = jnp.concatenate([own_row(0, 0), high], axis=1)
        weight = jnp.concatenate([own_row(0, peers), own_row(1, peers)], axis=1)
        slot_at = lax.broadcasted_iota(jnp.int32, (slots, 2 * tokens), 0).astype(jnp.float32)
        pick = jnp.where(slot_at == slot_of, 1.0, 0.0)
        slot_weight = jnp.sum(pick * weight, axis=1, keepdims=True)
        pick16 = pick.astype(jnp.bfloat16)
        hidden = hidden_ref[where, :]
        weighted = (slot_weight * low_in[where, :].astype(jnp.float32)).astype(jnp.bfloat16)
        mixed = dot(weighted, pick16, (0, 0)).astype(jnp.bfloat16)
        both = jnp.concatenate([pick16, mixed], axis=0)
        wide[...] = jnp.zeros_like(wide)
        thin[...] = jnp.zeros_like(thin)

        return which, where, hidden, pick, slot_weight, both

    def strip_step(state, at):
        which, both = state[0], state[-1]
        lanes = pl.ds(pl.multiple_of(at * strip, strip), strip)
        block = gathered[which, :, :, lanes].reshape(2 * tokens, strip)
        product = dot(both, block, (1, 0))
        slot_rows = product[:slots].astype(jnp.bfloat16)
        second_out[:, lanes] += adapter_scale * product[slots:]
        wide[...] += dot(slot_rows, down[:, lanes], (1, 1))
        thin[...] += dot(slot_rows, second_ref[:, lanes], (1, 1))

    def finish(state):
        which, where, hidden, pick, slot_weight, _ = state
        low = thin[...]
        total = wide[...] + adapter_scale * dot(low.astype(jnp.bfloat16), first_ref[...], (1, 0))
        out_ref[where, :] = (slot_weight * total).astype(jnp.bfloat16)
        out_copy(which).start()
        low_grad = (slot_weight * low).astype(jnp.bfloat16)
        first_out[...] += adapter_scale * dot(low_grad, hidden, (0, 0))
        router = jnp.sum(hidden.astype(jnp.float32) * total, axis=1, keepdims=True)
        routed = jnp.sum(pick * router, axis=0, keepdims=True)
        router_send[2 * which] = jnp.broadcast_to(routed[:, :tokens], (8, tokens))
        router_send[2 * which + 1] = jnp.broadcast_to(routed[:, tokens:], (8, tokens))

    def work(which):
        state = begin(which)

        def each(at, carry):
            strip_step(state, at)
            return carry

        lax.fori_loop(0, parts, each, 0)
        finish(state)

    def send_back(which):
        back_copy(2 * which).start()
        back_copy(2 * which + 1).start()

    def work_and_return(which):
        work(which)
        send_back(which)

    def wait_left(step, count):
        for k in range(parts * step, parts * step + count):
            pair_left(k, 1 - core).wait_recv()
        if count == parts:
            meta_pair(1 + step, place - 1 - step, 1 - core).wait_recv()

    def wait_right(step, count):
        for k in range(parts * step, parts * step + count):
            pair_right(k, 1 - core).wait_recv()
        if count == parts:
            meta_pair(1 + far + step, place + 1 + step, 1 - core).wait_recv()

    for k in range(last + 1):
        if k % parts == 0:
            step = k // parts
            meta_right(step, place - 1 - step).wait_recv()
            if step + 1 < far:
                meta_right(step + 1, place - 1 - step).start()
            meta_pair(1 + step, place - 1 - step, core).start()
            if step + 1 < far:
                meta_left(step, place + 1 + step).wait_recv()
                if step + 2 < far:
                    meta_left(step + 1, place + 1 + step).start()
                meta_pair(1 + far + step, place + 1 + step, core).start()
        from_left(k).wait_recv()
        if k + parts <= last:
            send_right(k + parts).start()
        pair_left(k, core).start()
        from_right(k).wait_recv()
        if k + parts <= last:
            send_left(k + parts).start()
        pair_right(k, core).start()
        if k == 0:
            pair_copy(0, gathered.at[chip, 1 - core]).wait_recv()
            meta_pair(0, place, 1 - core).wait_recv()
            work(chip)
            back_copy(sibling).start()
            router_recv[me] = router_send[me]
        step = (k + 1) // parts - 1
        if k % parts == parts - 1:
            wait_left(step, parts)
            work_and_return(chip_at(place - 1 - step))
        if (k % parts == 0 and k > 0 and k < last) or (k + 1 == last and k % parts == parts - 1):
            if k % parts == 0:
                step = k // parts - 1
            wait_right(step, parts)
            work_and_return(chip_at(place + 1 + step))
        if k >= last + 1 - parts // 2:
            if k == last + 1 - parts // 2:
                meta_pair(far, place - far, 1 - core).wait_recv()
                final = begin(chip_at(place + far))
            pair_left(k, 1 - core).wait_recv()
            strip_step(final, k % parts)
            pair_right(k, 1 - core).wait_recv()
            strip_step(final, parts - 1 - k % parts)
    finish(final)
    send_back(chip_at(place + far))

    for k in range(last + 1):
        send_right(k).wait_send()
        send_left(k).wait_send()
        pair_left(k, core).wait_send()
        pair_right(k, core).wait_send()
    own_pair.wait_send()
    meta_pair(0, place, core).wait_send()
    for step in range(far):
        meta_right(step, place - step).wait_send()
        meta_pair(1 + step, place - 1 - step, core).wait_send()
        if step + 1 < far:
            meta_left(step, place + step).wait_send()
            meta_pair(1 + far + step, place + 1 + step, core).wait_send()

    def wait_back(ahead, carry):
        source = lax.rem(me + ahead, peers)
        pltpu.make_async_remote_copy(
            src_ref=router_send.at[source],
            dst_ref=router_recv.at[source],
            send_sem=back_send.at[source],
            recv_sem=back_got.at[source],
            **device(source),
        ).wait()
        return carry

    lax.fori_loop(1, peers, wait_back, 0)
    returned = router_recv[:, 0, :]
    for k in range(top):
        same = routes_ref[k : k + 1, :] == expert_at
        router_out[k : k + 1, :] = jnp.sum(jnp.where(same, returned, 0.0), axis=0, keepdims=True)
    for which in range(chips):
        out_copy(which).wait()


def store_kernel(*refs):
    sems = refs[8]
    copies = [pltpu.make_async_copy(refs[i], refs[4 + i], sems.at[i]) for i in range(4)]
    for copy in copies:
        copy.start()
    for copy in copies:
        copy.wait()


def ring_shards(
    output_gradient,
    router_weight_table,
    routes,
    hidden,
    down_weight_matrix,
    adapter_first_factor,
    adapter_second_factor,
):
    peers = lax.axis_size("expert")
    tokens, width = output_gradient.shape
    _, capacity, inner = hidden.shape
    rank = adapter_first_factor.shape[2]
    per_source = capacity // peers
    chips = peers // 2
    parts = 4
    steps = parts * (chips // 2 - 1) + parts // 2
    top = routes.shape[1]
    strip = width // parts
    vmem = pl.BlockSpec(memory_space=pltpu.VMEM)
    hbm = pl.BlockSpec(memory_space=pl.ANY)
    dma = pltpu.SemaphoreType.DMA
    small = (peers, 8, tokens)
    results = pl.pallas_call(
        functools.partial(ring_kernel, peers, per_source, strip, parts),
        out_shape=(
            jax.ShapeDtypeStruct((capacity, inner), jnp.bfloat16),
            jax.ShapeDtypeStruct((rank, inner), jnp.float32),
            jax.ShapeDtypeStruct((rank, width), jnp.float32),
            jax.ShapeDtypeStruct((top, tokens), jnp.float32),
        ),
        in_specs=[hbm, vmem, vmem, hbm, hbm, vmem, vmem],
        out_specs=(hbm, vmem, vmem, vmem),
        scratch_shapes=[
            pltpu.VMEM((chips, 2, tokens, width), jnp.bfloat16),
            pltpu.VMEM((inner, width), jnp.bfloat16),
            pltpu.VMEM((capacity, inner), jnp.bfloat16),
            pltpu.VMEM((capacity, inner), jnp.bfloat16),
            pltpu.VMEM((capacity, rank), jnp.bfloat16),
            pltpu.VMEM((2 * per_source, inner), jnp.float32),
            pltpu.VMEM((2 * per_source, rank), jnp.float32),
            pltpu.VMEM((chips, 2, 2 * peers, tokens), jnp.float32),
            pltpu.VMEM(small, jnp.float32),
            pltpu.VMEM(small, jnp.float32),
            dma((steps,)),
            dma((steps,)),
            dma((steps,)),
            dma((steps,)),
            dma((2 * steps + 1,)),
            dma((2 * steps + 1,)),
            dma((chips // 2,)),
            dma((chips // 2,)),
            dma((chips // 2,)),
            dma((chips // 2,)),
            dma((chips,)),
            dma((chips,)),
            dma((peers,)),
            dma((peers,)),
            dma((3,)),
            dma((chips,)),
        ],
        compiler_params=pltpu.CompilerParams(
            collective_id=0, has_side_effects=True, vmem_limit_bytes=56 * MIB
        ),
    )(
        output_gradient,
        router_weight_table.T,
        routes.T,
        hidden[0],
        down_weight_matrix[0],
        adapter_first_factor[0].T,
        adapter_second_factor[0],
    )
    grad, first, second, router = pl.pallas_call(
        store_kernel,
        out_shape=[jax.ShapeDtypeStruct(r.shape, r.dtype) for r in results],
        in_specs=[vmem] * 4,
        out_specs=[hbm] * 4,
        scratch_shapes=[dma((4,))],
    )(*results)
    return grad[None], first.T[None], second[None], router.T


def ring_fits(peers, tokens_dev, width, experts, capacity, inner):
    per_source = capacity // peers
    gathered = peers * tokens_dev * width * 2
    return (
        experts == peers
        and peers >= 8
        and peers % 4 == 0
        and tokens_dev == 128
        and width % 512 == 0
        and inner % 128 == 0
        and (2 * per_source) % 16 == 0
        and gathered + inner * width * 2 + 3 * capacity * inner * 2 <= 40 * MIB
    )


def shards(
    output_gradient,
    router_weight_table,
    routes,
    hidden,
    down_weight_matrix,
    adapter_first_factor,
    adapter_second_factor,
):
    peer_count = lax.axis_size("expert")
    tokens_dev = output_gradient.shape[0]
    top_count = routes.shape[1]
    model_width = output_gradient.shape[1]
    exp_local = hidden.shape[0]
    capacity = hidden.shape[1]
    per_source = capacity // peer_count
    expert_count = exp_local * peer_count
    member = jnp.sum(
        (routes[:, :, None] == jnp.arange(expert_count, dtype=jnp.int32)).astype(jnp.bfloat16),
        axis=1,
    )
    lower_mask = (jnp.arange(tokens_dev)[:, None] > jnp.arange(tokens_dev)[None, :]).astype(
        jnp.bfloat16
    )
    before = jnp.dot(lower_mask, member, preferred_element_type=jnp.float32)
    position = jnp.take_along_axis(before, routes, axis=1).astype(jnp.int32)
    slot_index = (routes * per_source + position).reshape(-1)
    token_ids = jnp.repeat(jnp.arange(tokens_dev, dtype=jnp.int32), top_count)
    slot_token_index = (
        jnp.full((expert_count * per_source,), tokens_dev, jnp.int32).at[slot_index].set(token_ids)
    )
    slot_router_weight = (
        jnp.zeros((expert_count * per_source,), jnp.bfloat16)
        .at[slot_index]
        .set(router_weight_table.reshape(-1))
    )
    padded = jnp.concatenate(
        [output_gradient, jnp.zeros((1, model_width), output_gradient.dtype)], axis=0
    )
    send_rows = padded[slot_token_index]
    got_rows, got_weight = (
        lax.all_to_all(send_rows, "expert", split_axis=0, concat_axis=0, tiled=True),
        lax.all_to_all(slot_router_weight, "expert", split_axis=0, concat_axis=0, tiled=True),
    )
    slot_rows = (
        got_rows.reshape(peer_count, exp_local, per_source, model_width)
        .transpose(1, 0, 2, 3)
        .reshape(exp_local, capacity, model_width)
    )
    weight_rows = (
        got_weight.reshape(peer_count, exp_local, per_source)
        .transpose(1, 0, 2)
        .reshape(exp_local, capacity)
    )
    scaled_gradient = (
        weight_rows.astype(jnp.float32)[:, :, None] * slot_rows.astype(jnp.float32)
    ).astype(jnp.bfloat16)
    reduced_input = jnp.einsum(
        "onv,ovx->onx", hidden, adapter_first_factor, preferred_element_type=jnp.float32
    ).astype(jnp.bfloat16)
    joined_input = jnp.concatenate([hidden, reduced_input], axis=2)
    doubled_second = (adapter_scale * adapter_second_factor.astype(jnp.float32)).astype(
        jnp.bfloat16
    )
    joined_weight = jnp.concatenate([down_weight_matrix, doubled_second], axis=1)
    expert_out = jnp.einsum(
        "ecf,efd->ecd", joined_input, joined_weight, preferred_element_type=jnp.float32
    ).astype(jnp.bfloat16)
    partial_products = jnp.einsum(
        "ecd,ecd->ec", slot_rows, expert_out, preferred_element_type=jnp.float32
    )
    send_back = (
        partial_products.reshape(exp_local, peer_count, per_source).transpose(1, 0, 2).reshape(-1)
    )
    got_back = lax.all_to_all(send_back, "expert", split_axis=0, concat_axis=0, tiled=True)
    router_weight_gradient = got_back[slot_index].reshape(tokens_dev, top_count)
    reduced_gradient = jnp.einsum(
        "wzg,wvg->wzv", scaled_gradient, adapter_second_factor, preferred_element_type=jnp.float32
    ).astype(jnp.bfloat16)
    hidden_input_gradient = (
        jnp.einsum(
            "ecd,efd->ecf", scaled_gradient, down_weight_matrix, preferred_element_type=jnp.float32
        )
        + adapter_scale
        * jnp.einsum(
            "uvi,ubi->uvb",
            reduced_gradient,
            adapter_first_factor,
            preferred_element_type=jnp.float32,
        )
    ).astype(jnp.bfloat16)
    adapter_first_gradient = adapter_scale * jnp.einsum(
        "ecf,ecr->efr", hidden, reduced_gradient, preferred_element_type=jnp.float32
    )
    adapter_second_gradient = adapter_scale * jnp.einsum(
        "ecr,ecd->erd", reduced_input, scaled_gradient, preferred_element_type=jnp.float32
    )
    return (
        hidden_input_gradient,
        adapter_first_gradient,
        adapter_second_gradient,
        router_weight_gradient,
    )


def solution(mesh):
    in_specs = (
        P("expert", "groups"),
        P("expert", "groups"),
        P("expert", "groups"),
        P("expert", "groups", None),
        P("expert", None, None),
        P("expert", None, None),
        P("expert", None, None),
    )
    out_specs = (
        P("expert", "groups", None),
        P("expert", "groups", None),
        P("expert", "groups", None),
        P("expert", "groups"),
    )

    def call(*arrays):
        peers = mesh.shape["expert"]
        groups = mesh.shape["groups"]
        gradient, hidden = arrays[0], arrays[3]
        fits = ring_fits(
            peers,
            gradient.shape[0] // peers,
            gradient.shape[1] // groups,
            hidden.shape[0],
            hidden.shape[1] // groups,
            hidden.shape[2],
        )
        body = ring_shards if fits else shards
        return jax.shard_map(
            body, mesh=mesh, in_specs=in_specs, out_specs=out_specs, check_vma=False
        )(*arrays)

    return call
```

```python
import functools

import jax
import jax.numpy as jnp
from jax import lax
from jax.experimental import pallas as pl
from jax.experimental.pallas import tpu as pltpu
from jax.sharding import PartitionSpec as P

adapter_scale = 2.0
MIB = 1 << 20


def dot(a, b, dims):
    return lax.dot_general(a, b, ((dims[:1], dims[1:]), ((), ())), preferred_element_type=jnp.float32)


def ring_kernel(
    peers,
    per_source,
    strip,
    parts,
    grad_hbm,
    weight_ref,
    routes_ref,
    hidden_hbm,
    down_hbm,
    first_ref,
    second_ref,
    out_hbm,
    first_out,
    second_out,
    router_out,
    gathered,
    down,
    hidden_ref,
    out_ref,
    low_in,
    wide,
    thin,
    meta,
    router_send,
    router_recv,
    right_send,
    right_recv,
    left_send,
    left_recv,
    pair_send,
    pair_recv,
    meta_right_send,
    meta_right_recv,
    meta_left_send,
    meta_left_recv,
    meta_pair_send,
    meta_pair_recv,
    back_send,
    back_got,
    local_sem,
    out_sem,
):
    tokens, width = grad_hbm.shape
    inner = hidden_ref.shape[1]
    top = routes_ref.shape[0]
    piece = width // parts
    chips = peers // 2
    side = chips // 2
    slots = 2 * per_source
    far = chips // 2
    last = parts * (far - 1) + parts // 2 - 1

    me = lax.axis_index("expert")
    core = lax.rem(me, 2)
    chip = lax.div(me, 2)
    row, column = lax.div(chip, 2), lax.rem(chip, 2)
    place = row + column * (chips - 1 - 2 * row)

    def chip_at(position):
        position = lax.rem(position + chips, chips)
        col = lax.div(position, side)
        return 2 * (position + col * (chips - 1 - 2 * position)) + col

    def device(index):
        return dict(device_id={"expert": index}, device_id_type=pl.DeviceIdType.MESH)

    right = 2 * chip_at(place + 1) + core
    left = 2 * chip_at(place - 1) + core
    sibling = chip * 2 + 1 - core

    barrier = pltpu.get_barrier_semaphore()
    for other in (right, left, sibling):
        pl.semaphore_signal(barrier, inc=1, **device(other))

    down_copy = pltpu.make_async_copy(down_hbm, down, local_sem.at[0])
    down_copy.start()
    own_copy = pltpu.make_async_copy(grad_hbm, gathered.at[chip, core], local_sem.at[1])
    own_copy.start()
    hidden_copy = pltpu.make_async_copy(hidden_hbm, hidden_ref, local_sem.at[2])
    hidden_copy.start()

    expert_at = lax.broadcasted_iota(jnp.int32, (peers, tokens), 0)
    member = jnp.zeros((peers, tokens), jnp.float32)
    weights = jnp.zeros((peers, tokens), jnp.float32)
    for k in range(top):
        same = routes_ref[k : k + 1, :] == expert_at
        member += jnp.where(same, 1.0, 0.0)
        weights += jnp.where(same, weight_ref[k : k + 1, :].astype(jnp.float32), 0.0)
    at0 = lax.broadcasted_iota(jnp.int32, (tokens, tokens), 0)
    at1 = lax.broadcasted_iota(jnp.int32, (tokens, tokens), 1)
    earlier = jnp.where(at0 < at1, 1.0, 0.0).astype(jnp.bfloat16)
    before = dot(member.astype(jnp.bfloat16), earlier, (1, 0))
    position = jnp.where(member > 0.5, before, -1.0)
    meta[chip, core] = jnp.concatenate([position, weights], axis=0)

    pl.semaphore_wait(barrier, 3)

    def lanes_of(chunk):
        return pl.ds(chunk * piece, piece)

    def send_right(k):
        step, chunk = k // parts, k % parts
        target = gathered.at[chip_at(place - step), core, :, lanes_of(chunk)]
        return pltpu.make_async_remote_copy(
            src_ref=grad_hbm.at[:, lanes_of(chunk)] if step == 0 else target,
            dst_ref=target,
            send_sem=right_send.at[k],
            recv_sem=right_recv.at[k],
            **device(right),
        )

    def send_left(k):
        step, chunk = k // parts, parts - 1 - k % parts
        target = gathered.at[chip_at(place + step), core, :, lanes_of(chunk)]
        return pltpu.make_async_remote_copy(
            src_ref=grad_hbm.at[:, lanes_of(chunk)] if step == 0 else target,
            dst_ref=target,
            send_sem=left_send.at[k],
            recv_sem=left_recv.at[k],
            **device(left),
        )

    def from_left(k):
        block = gathered.at[chip_at(place - 1 - k // parts), core, :, lanes_of(k % parts)]
        return pltpu.make_async_remote_copy(
            src_ref=block, dst_ref=block, send_sem=right_send.at[k], recv_sem=right_recv.at[k],
            **device(left),
        )

    def from_right(k):
        block = gathered.at[chip_at(place + 1 + k // parts), core, :, lanes_of(parts - 1 - k % parts)]
        return pltpu.make_async_remote_copy(
            src_ref=block, dst_ref=block, send_sem=left_send.at[k], recv_sem=left_recv.at[k],
            **device(right),
        )

    def pair_copy(number, block, source=None):
        return pltpu.make_async_remote_copy(
            src_ref=block if source is None else source,
            dst_ref=block,
            send_sem=pair_send.at[number],
            recv_sem=pair_recv.at[number],
            **device(sibling),
        )

    def pair_left(k, at_core):
        block = gathered.at[chip_at(place - 1 - k // parts), at_core, :, lanes_of(k % parts)]
        return pair_copy(1 + k, block)

    def pair_right(k, at_core):
        block = gathered.at[chip_at(place + 1 + k // parts), at_core, :, lanes_of(parts - 1 - k % parts)]
        return pair_copy(2 + last + k, block)

    def meta_copy(block, send, recv, target):
        return pltpu.make_async_remote_copy(
            src_ref=block, dst_ref=block, send_sem=send, recv_sem=recv, **device(target)
        )

    def meta_right(step, origin):
        block = meta.at[chip_at(origin), core]
        return meta_copy(block, meta_right_send.at[step], meta_right_recv.at[step], right)

    def meta_left(step, origin):
        block = meta.at[chip_at(origin), core]
        return meta_copy(block, meta_left_send.at[step], meta_left_recv.at[step], left)

    def meta_pair(number, origin, at_core):
        block = meta.at[chip_at(origin), at_core]
        return meta_copy(block, meta_pair_send.at[number], meta_pair_recv.at[number], sibling)

    meta_right(0, place).start()
    meta_left(0, place).start()
    meta_pair(0, place, core).start()
    for k in range(parts):
        send_right(k).start()
        send_left(k).start()
    own_pair = pair_copy(0, gathered.at[chip, core], grad_hbm)
    own_pair.start()

    first_out[...] = jnp.zeros_like(first_out)
    second_out[...] = jnp.zeros_like(second_out)
    hidden_copy.wait()
    low_in[...] = dot(hidden_ref[...], first_ref[...], (1, 1)).astype(jnp.bfloat16)

    down_copy.wait()
    own_copy.wait()

    def back_copy(target):
        return pltpu.make_async_remote_copy(
            src_ref=router_send.at[target],
            dst_ref=router_recv.at[me],
            send_sem=back_send.at[target],
            recv_sem=back_got.at[me],
            **device(target),
        )

    def out_copy(which):
        where = pl.ds(pl.multiple_of(which * slots, 16), slots)
        return pltpu.make_async_copy(out_ref.at[where, :], out_hbm.at[where, :], out_sem.at[which])

    def send_back(which):
        back_copy(2 * which).start()
        back_copy(2 * which + 1).start()

    def begin(which):
        where = pl.ds(pl.multiple_of(which * slots, 16), slots)
        mine = lax.broadcasted_iota(jnp.int32, (peers, tokens), 0) == me

        def own_row(at_core, start):
            table = meta[which, at_core, start : start + peers, :]
            return jnp.sum(jnp.where(mine, table, 0.0), axis=0, keepdims=True)

        high = own_row(1, 0)
        high = jnp.where(high < 0.0, -1.0, high + float(per_source))
        slot_of = jnp.concatenate([own_row(0, 0), high], axis=1)
        weight = jnp.concatenate([own_row(0, peers), own_row(1, peers)], axis=1)
        slot_at = lax.broadcasted_iota(jnp.int32, (slots, 2 * tokens), 0).astype(jnp.float32)
        pick = jnp.where(slot_at == slot_of, 1.0, 0.0)
        slot_weight = jnp.sum(pick * weight, axis=1, keepdims=True)
        pick16 = pick.astype(jnp.bfloat16)
        hidden = hidden_ref[where, :]
        weighted = (slot_weight * low_in[where, :].astype(jnp.float32)).astype(jnp.bfloat16)
        mixed = dot(weighted, pick16, (0, 0)).astype(jnp.bfloat16)
        both = jnp.concatenate([pick16, mixed], axis=0)
        wide[...] = jnp.zeros_like(wide)
        thin[...] = jnp.zeros_like(thin)

        return which, where, hidden, pick, slot_weight, both

    def strip_step(state, at):
        which, both = state[0], state[-1]
        lanes = pl.ds(pl.multiple_of(at * strip, strip), strip)
        block = gathered[which, :, :, lanes].reshape(2 * tokens, strip)
        product = dot(both, block, (1, 0))
        slot_rows = product[:slots].astype(jnp.bfloat16)
        second_out[:, lanes] += adapter_scale * product[slots:]
        wide[...] += dot(slot_rows, down[:, lanes], (1, 1))
        thin[...] += dot(slot_rows, second_ref[:, lanes], (1, 1))

    def finish(state, own=False):
        which, where, hidden, pick, slot_weight, _ = state
        low = thin[...]
        total = wide[...] + adapter_scale * dot(low.astype(jnp.bfloat16), first_ref[...], (1, 0))
        router = jnp.sum(hidden.astype(jnp.float32) * total, axis=1, keepdims=True)
        routed = jnp.sum(pick * router, axis=0, keepdims=True)
        router_send[2 * which] = jnp.broadcast_to(routed[:, :tokens], (8, tokens))
        router_send[2 * which + 1] = jnp.broadcast_to(routed[:, tokens:], (8, tokens))
        if own:
            back_copy(sibling).start()
            router_recv[me] = router_send[me]
        else:
            send_back(which)
        out_ref[where, :] = (slot_weight * total).astype(jnp.bfloat16)
        out_copy(which).start()
        low_grad = (slot_weight * low).astype(jnp.bfloat16)
        first_out[...] += adapter_scale * dot(low_grad, hidden, (0, 0))

    def work(which, own=False):
        state = begin(which)

        def each(at, carry):
            strip_step(state, at)
            return carry

        lax.fori_loop(0, parts, each, 0)
        finish(state, own)

    def wait_left(step, count):
        for k in range(parts * step, parts * step + count):
            pair_left(k, 1 - core).wait_recv()
        if count == parts:
            meta_pair(1 + step, place - 1 - step, 1 - core).wait_recv()

    def wait_right(step, count):
        for k in range(parts * step, parts * step + count):
            pair_right(k, 1 - core).wait_recv()
        if count == parts:
            meta_pair(1 + far + step, place + 1 + step, 1 - core).wait_recv()

    pair_copy(0, gathered.at[chip, 1 - core]).wait_recv()
    meta_pair(0, place, 1 - core).wait_recv()
    work(chip, own=True)

    for k in range(last + 1):
        if k % parts == 0:
            step = k // parts
            meta_right(step, place - 1 - step).wait_recv()
            if step + 1 < far:
                meta_right(step + 1, place - 1 - step).start()
            meta_pair(1 + step, place - 1 - step, core).start()
            if step + 1 < far:
                meta_left(step, place + 1 + step).wait_recv()
                if step + 2 < far:
                    meta_left(step + 1, place + 1 + step).start()
                meta_pair(1 + far + step, place + 1 + step, core).start()
        from_left(k).wait_recv()
        if k + parts <= last:
            send_right(k + parts).start()
        pair_left(k, core).start()
        from_right(k).wait_recv()
        if k + parts <= last:
            send_left(k + parts).start()
        pair_right(k, core).start()
        step = (k + 1) // parts - 1
        if k % parts == parts - 1:
            wait_left(step, parts)
            work(chip_at(place - 1 - step))
        if (k % parts == 0 and k > 0 and k < last) or (k + 1 == last and k % parts == parts - 1):
            if k % parts == 0:
                step = k // parts - 1
            wait_right(step, parts)
            work(chip_at(place + 1 + step))
        if k >= last + 1 - parts // 2:
            if k == last + 1 - parts // 2:
                meta_pair(far, place - far, 1 - core).wait_recv()
                final = begin(chip_at(place + far))
            pair_left(k, 1 - core).wait_recv()
            strip_step(final, k % parts)
            pair_right(k, 1 - core).wait_recv()
            strip_step(final, parts - 1 - k % parts)
    finish(final)

    for k in range(last + 1):
        send_right(k).wait_send()
        send_left(k).wait_send()
        pair_left(k, core).wait_send()
        pair_right(k, core).wait_send()
    own_pair.wait_send()
    meta_pair(0, place, core).wait_send()
    for step in range(far):
        meta_right(step, place - step).wait_send()
        meta_pair(1 + step, place - 1 - step, core).wait_send()
        if step + 1 < far:
            meta_left(step, place + step).wait_send()
            meta_pair(1 + far + step, place + 1 + step, core).wait_send()

    def wait_back(ahead, carry):
        source = lax.rem(me + ahead, peers)
        pltpu.make_async_remote_copy(
            src_ref=router_send.at[source],
            dst_ref=router_recv.at[source],
            send_sem=back_send.at[source],
            recv_sem=back_got.at[source],
            **device(source),
        ).wait()
        return carry

    lax.fori_loop(1, peers, wait_back, 0)
    returned = router_recv[:, 0, :]
    for k in range(top):
        same = routes_ref[k : k + 1, :] == expert_at
        router_out[k : k + 1, :] = jnp.sum(jnp.where(same, returned, 0.0), axis=0, keepdims=True)
    for which in range(chips):
        out_copy(which).wait()


def store_kernel(*refs):
    sems = refs[8]
    copies = [pltpu.make_async_copy(refs[i], refs[4 + i], sems.at[i]) for i in range(4)]
    for copy in copies:
        copy.start()
    for copy in copies:
        copy.wait()


def ring_shards(
    output_gradient,
    router_weight_table,
    routes,
    hidden,
    down_weight_matrix,
    adapter_first_factor,
    adapter_second_factor,
):
    peers = lax.axis_size("expert")
    tokens, width = output_gradient.shape
    _, capacity, inner = hidden.shape
    rank = adapter_first_factor.shape[2]
    per_source = capacity // peers
    chips = peers // 2
    parts = 4
    steps = parts * (chips // 2 - 1) + parts // 2
    top = routes.shape[1]
    strip = width // parts
    vmem = pl.BlockSpec(memory_space=pltpu.VMEM)
    hbm = pl.BlockSpec(memory_space=pl.ANY)
    dma = pltpu.SemaphoreType.DMA
    small = (peers, 8, tokens)
    results = pl.pallas_call(
        functools.partial(ring_kernel, peers, per_source, strip, parts),
        out_shape=(
            jax.ShapeDtypeStruct((capacity, inner), jnp.bfloat16),
            jax.ShapeDtypeStruct((rank, inner), jnp.float32),
            jax.ShapeDtypeStruct((rank, width), jnp.float32),
            jax.ShapeDtypeStruct((top, tokens), jnp.float32),
        ),
        in_specs=[hbm, vmem, vmem, hbm, hbm, vmem, vmem],
        out_specs=(hbm, vmem, vmem, vmem),
        scratch_shapes=[
            pltpu.VMEM((chips, 2, tokens, width), jnp.bfloat16),
            pltpu.VMEM((inner, width), jnp.bfloat16),
            pltpu.VMEM((capacity, inner), jnp.bfloat16),
            pltpu.VMEM((capacity, inner), jnp.bfloat16),
            pltpu.VMEM((capacity, rank), jnp.bfloat16),
            pltpu.VMEM((2 * per_source, inner), jnp.float32),
            pltpu.VMEM((2 * per_source, rank), jnp.float32),
            pltpu.VMEM((chips, 2, 2 * peers, tokens), jnp.float32),
            pltpu.VMEM(small, jnp.float32),
            pltpu.VMEM(small, jnp.float32),
            dma((steps,)),
            dma((steps,)),
            dma((steps,)),
            dma((steps,)),
            dma((2 * steps + 1,)),
            dma((2 * steps + 1,)),
            dma((chips // 2,)),
            dma((chips // 2,)),
            dma((chips // 2,)),
            dma((chips // 2,)),
            dma((chips,)),
            dma((chips,)),
            dma((peers,)),
            dma((peers,)),
            dma((3,)),
            dma((chips,)),
        ],
        compiler_params=pltpu.CompilerParams(
            collective_id=0, has_side_effects=True, vmem_limit_bytes=56 * MIB
        ),
    )(
        output_gradient,
        router_weight_table.T,
        routes.T,
        hidden[0],
        down_weight_matrix[0],
        adapter_first_factor[0].T,
        adapter_second_factor[0],
    )
    grad, first, second, router = pl.pallas_call(
        store_kernel,
        out_shape=[jax.ShapeDtypeStruct(r.shape, r.dtype) for r in results],
        in_specs=[vmem] * 4,
        out_specs=[hbm] * 4,
        scratch_shapes=[dma((4,))],
    )(*results)
    return grad[None], first.T[None], second[None], router.T


def ring_fits(peers, tokens_dev, width, experts, capacity, inner):
    per_source = capacity // peers
    gathered = peers * tokens_dev * width * 2
    return (
        experts == peers
        and peers >= 8
        and peers % 4 == 0
        and tokens_dev == 128
        and width % 512 == 0
        and inner % 128 == 0
        and (2 * per_source) % 16 == 0
        and gathered + inner * width * 2 + 3 * capacity * inner * 2 <= 40 * MIB
    )


def shards(
    output_gradient,
    router_weight_table,
    routes,
    hidden,
    down_weight_matrix,
    adapter_first_factor,
    adapter_second_factor,
):
    peer_count = lax.axis_size("expert")
    tokens_dev = output_gradient.shape[0]
    top_count = routes.shape[1]
    model_width = output_gradient.shape[1]
    exp_local = hidden.shape[0]
    capacity = hidden.shape[1]
    per_source = capacity // peer_count
    expert_count = exp_local * peer_count
    member = jnp.sum(
        (routes[:, :, None] == jnp.arange(expert_count, dtype=jnp.int32)).astype(jnp.bfloat16),
        axis=1,
    )
    lower_mask = (jnp.arange(tokens_dev)[:, None] > jnp.arange(tokens_dev)[None, :]).astype(
        jnp.bfloat16
    )
    before = jnp.dot(lower_mask, member, preferred_element_type=jnp.float32)
    position = jnp.take_along_axis(before, routes, axis=1).astype(jnp.int32)
    slot_index = (routes * per_source + position).reshape(-1)
    token_ids = jnp.repeat(jnp.arange(tokens_dev, dtype=jnp.int32), top_count)
    slot_token_index = (
        jnp.full((expert_count * per_source,), tokens_dev, jnp.int32).at[slot_index].set(token_ids)
    )
    slot_router_weight = (
        jnp.zeros((expert_count * per_source,), jnp.bfloat16)
        .at[slot_index]
        .set(router_weight_table.reshape(-1))
    )
    padded = jnp.concatenate(
        [output_gradient, jnp.zeros((1, model_width), output_gradient.dtype)], axis=0
    )
    send_rows = padded[slot_token_index]
    got_rows, got_weight = (
        lax.all_to_all(send_rows, "expert", split_axis=0, concat_axis=0, tiled=True),
        lax.all_to_all(slot_router_weight, "expert", split_axis=0, concat_axis=0, tiled=True),
    )
    slot_rows = (
        got_rows.reshape(peer_count, exp_local, per_source, model_width)
        .transpose(1, 0, 2, 3)
        .reshape(exp_local, capacity, model_width)
    )
    weight_rows = (
        got_weight.reshape(peer_count, exp_local, per_source)
        .transpose(1, 0, 2)
        .reshape(exp_local, capacity)
    )
    scaled_gradient = (
        weight_rows.astype(jnp.float32)[:, :, None] * slot_rows.astype(jnp.float32)
    ).astype(jnp.bfloat16)
    reduced_input = jnp.einsum(
        "onv,ovx->onx", hidden, adapter_first_factor, preferred_element_type=jnp.float32
    ).astype(jnp.bfloat16)
    joined_input = jnp.concatenate([hidden, reduced_input], axis=2)
    doubled_second = (adapter_scale * adapter_second_factor.astype(jnp.float32)).astype(
        jnp.bfloat16
    )
    joined_weight = jnp.concatenate([down_weight_matrix, doubled_second], axis=1)
    expert_out = jnp.einsum(
        "ecf,efd->ecd", joined_input, joined_weight, preferred_element_type=jnp.float32
    ).astype(jnp.bfloat16)
    partial_products = jnp.einsum(
        "ecd,ecd->ec", slot_rows, expert_out, preferred_element_type=jnp.float32
    )
    send_back = (
        partial_products.reshape(exp_local, peer_count, per_source).transpose(1, 0, 2).reshape(-1)
    )
    got_back = lax.all_to_all(send_back, "expert", split_axis=0, concat_axis=0, tiled=True)
    router_weight_gradient = got_back[slot_index].reshape(tokens_dev, top_count)
    reduced_gradient = jnp.einsum(
        "wzg,wvg->wzv", scaled_gradient, adapter_second_factor, preferred_element_type=jnp.float32
    ).astype(jnp.bfloat16)
    hidden_input_gradient = (
        jnp.einsum(
            "ecd,efd->ecf", scaled_gradient, down_weight_matrix, preferred_element_type=jnp.float32
        )
        + adapter_scale
        * jnp.einsum(
            "uvi,ubi->uvb",
            reduced_gradient,
            adapter_first_factor,
            preferred_element_type=jnp.float32,
        )
    ).astype(jnp.bfloat16)
    adapter_first_gradient = adapter_scale * jnp.einsum(
        "ecf,ecr->efr", hidden, reduced_gradient, preferred_element_type=jnp.float32
    )
    adapter_second_gradient = adapter_scale * jnp.einsum(
        "ecr,ecd->erd", reduced_input, scaled_gradient, preferred_element_type=jnp.float32
    )
    return (
        hidden_input_gradient,
        adapter_first_gradient,
        adapter_second_gradient,
        router_weight_gradient,
    )


def solution(mesh):
    in_specs = (
        P("expert", "groups"),
        P("expert", "groups"),
        P("expert", "groups"),
        P("expert", "groups", None),
        P("expert", None, None),
        P("expert", None, None),
        P("expert", None, None),
    )
    out_specs = (
        P("expert", "groups", None),
        P("expert", "groups", None),
        P("expert", "groups", None),
        P("expert", "groups"),
    )

    def call(*arrays):
        peers = mesh.shape["expert"]
        groups = mesh.shape["groups"]
        gradient, hidden = arrays[0], arrays[3]
        fits = ring_fits(
            peers,
            gradient.shape[0] // peers,
            gradient.shape[1] // groups,
            hidden.shape[0],
            hidden.shape[1] // groups,
            hidden.shape[2],
        )
        body = ring_shards if fits else shards
        return jax.shard_map(
            body, mesh=mesh, in_specs=in_specs, out_specs=out_specs, check_vma=False
        )(*arrays)

    return call
```
